32 devices in a mesh: ctx: 8 (over y, x, core), head: 4 (over z).
Axes of the slice: x: 2, y: 2, z: 4, core: 2. Of those that a mesh axis runs over, the one named last changes fastest.
Arguments:
- tokens: bfloat16 [1024, 8192], P('ctx', 'head'), may hold values from -6 to 6
- norm_gain: float32 [8192], replicated, may hold values from 0.1 to 1.9
- query_weight: bfloat16 [8192, 8192], P(None, 'head'), may hold values from -0.0625 to 0.0625
- key_weight: bfloat16 [8192, 1024], P(None, 'head'), may hold values from -0.0625 to 0.0625
- value_weight: bfloat16 [8192, 1024], P(None, 'head'), may hold values from -0.0625 to 0.0625
- cache_keys: bfloat16 [8192, 1024], P('ctx', 'head'), may hold values from -200 to 200
- cache_values: bfloat16 [8192, 1024], P('ctx', 'head'), may hold values from -6 to 6
- cache_lengths: int32 [8], replicated, may hold values from 2 to 1024, as said below
- start_position: int32 [1], replicated, may hold values from 1 to 8192
Outputs:
- attended: bfloat16 [1024, 8192], P('ctx', 'head')
The draws below stay inside these ranges and needn't reach their ends.
Inputs may be any that keep to these rules, and one draw needn't show every extreme that they name: `cache_lengths`: entry c counts the live rows of cache shard c from its first row; some shard is full.
All inputs are finite; a program needn't handle non-finite values.
Results may differ from the reference program's by a relative error of at most 0.015.
The reference program's roundings to bfloat16 on the way count: a program that leaves them out, or rounds other values in their place, can miss the bound.
Values may be sent and summed in bfloat16 or wider, within the bound.
A program may use at most 192 MiB of HBM per device.

```python
import jax
import jax.numpy as jnp
from jax import lax

D = 8192
HEADS = 64
KV_HEADS = 8
HEAD_DIM = 128
TOK_DEV = 128
CACHE_DEV = 1024
SHARDS = 8
TOKENS = 1024
CACHE = 8192


def draw_cache_lengths(key, part):
    drawn = jax.random.randint(key, (SHARDS,), 2, CACHE_DEV + 1, dtype=jnp.int32)
    chosen = jax.random.randint(jax.random.fold_in(key, 5), (), 0, SHARDS, dtype=jnp.int32)
    return jnp.where(jnp.arange(SHARDS, dtype=jnp.int32) == chosen, CACHE_DEV, drawn).astype(jnp.int32)


def draw_cache_keys(key, part):
    width = KV_HEADS * HEAD_DIM
    return jnp.clip(jax.random.normal(key, (CACHE, width), jnp.float32), -6.0, 6.0).astype(jnp.bfloat16)


def block_scale(rng, dims, pieces, least, largest):
    def one(dim, blocks):
        steps = jax.random.uniform(jax.random.fold_in(jax.random.fold_in(rng, 6), dim), (blocks,), jnp.float32, least / len(pieces), largest / len(pieces))
        return jnp.repeat(jnp.exp(steps), dims[dim] // blocks).reshape((-1,) + (1,) * (len(dims) - dim - 1))

    factor_of = one(*pieces[0])
    for cut in pieces[1:]:
        factor_of = factor_of * one(*cut)
    return factor_of


def scatter_about(key, extent, scale, most, pieces=(), kind=jnp.bfloat16):
    loudness = block_scale(key, extent, pieces, -0.22, 0.18) if pieces else 1.0
    array = jax.random.normal(key, extent, jnp.float32) * scale * loudness
    return jnp.minimum(jnp.maximum(array, -most), most).astype(kind)


def setup_inputs(seed: int = 0) -> dict:
    keys = jax.random.split(jax.random.key(seed), 10)
    tokens = scatter_about(keys[0], (TOKENS, D), 1.0, 6.0, ((0, 8), (1, 4)))
    norm_gain = jnp.clip(1.0 + 0.18 * jax.random.normal(keys[1], (D,), jnp.float32), 0.1, 1.9)
    query_weight = scatter_about(keys[2], (D, HEADS * HEAD_DIM), D ** -0.5, 0.0625, ((1, 4),))
    key_weight = scatter_about(keys[3], (D, KV_HEADS * HEAD_DIM), D ** -0.5, 0.0625, ((1, 4),))
    value_weight = scatter_about(keys[4], (D, KV_HEADS * HEAD_DIM), D ** -0.5, 0.0625, ((1, 4),))
    cache_keys = draw_cache_keys(jax.random.fold_in(keys[9], 71), 0)
    cache_values = scatter_about(keys[6], (CACHE, KV_HEADS * HEAD_DIM), 1.0, 6.0, ((0, 8), (1, 4)))
    cache_lengths = draw_cache_lengths(jax.random.fold_in(keys[9], 71), 0)
    start_position = jax.random.randint(keys[8], (1,), 1, CACHE + 1).astype(jnp.int32)
    return dict(tokens=tokens, norm_gain=norm_gain, query_weight=query_weight, key_weight=key_weight, value_weight=value_weight, cache_keys=cache_keys, cache_values=cache_values, cache_lengths=cache_lengths, start_position=start_position)


epsilon = 1e-05
rope_base = 500000.0
masked_score = -1e+30

def rotary(inputs, position):
    half = inputs.shape[-1] // 2
    freqs = jnp.power(jnp.float32(rope_base), -2.0 * jnp.arange(half, dtype=jnp.float32) / inputs.shape[-1])
    angles = position[:, None] * freqs[None, :]
    cosine = jnp.cos(angles)[:, None, :]
    sine = jnp.sin(angles)[:, None, :]
    first_half = inputs[..., :half]
    second_half = inputs[..., half:]
    return jnp.concatenate([first_half * cosine - second_half * sine, second_half * cosine + first_half * sine], -1)

def reference(tokens, norm_gain, query_weight, key_weight, value_weight, cache_keys, cache_values, cache_lengths, start_position):
    floats = tokens.astype(jnp.float32)
    inverse = lax.rsqrt(lax.optimization_barrier(jnp.mean(floats * floats, -1, keepdims=True)) + epsilon)
    normed = (floats * inverse * norm_gain).astype(jnp.bfloat16)
    position = (start_position[0] + jnp.arange(TOKENS, dtype=jnp.int32)).astype(jnp.float32)
    projected = jnp.dot(normed, query_weight, preferred_element_type=jnp.float32)
    queries = rotary(projected.reshape(TOKENS, HEADS, HEAD_DIM), position).astype(jnp.bfloat16)
    key_proj = jnp.dot(normed, key_weight, preferred_element_type=jnp.float32)
    fresh_keys = rotary(key_proj.reshape(TOKENS, KV_HEADS, HEAD_DIM), position).astype(jnp.bfloat16)
    fresh_values = jnp.dot(normed, value_weight, preferred_element_type=jnp.float32).astype(jnp.bfloat16)
    fresh_values = fresh_values.reshape(TOKENS, KV_HEADS, HEAD_DIM)
    cache_live = jnp.arange(CACHE_DEV, dtype=jnp.int32)[None, :] < cache_lengths[:, None]
    group = HEADS // KV_HEADS
    cache_key_heads = cache_keys.reshape(SHARDS, CACHE_DEV, KV_HEADS, HEAD_DIM).transpose(2, 0, 1, 3)
    cache_value_heads = cache_values.reshape(SHARDS, CACHE_DEV, KV_HEADS, HEAD_DIM).transpose(2, 0, 1, 3)
    fresh_key_heads = fresh_keys.transpose(1, 0, 2)
    fresh_value_heads = fresh_values.transpose(1, 0, 2)
    grouped = queries.reshape(SHARDS, TOK_DEV, KV_HEADS, group, HEAD_DIM).transpose(2, 0, 1, 3, 4)

    def per_head(inputs):
        head_queries, ckeys, cvalues, fkeys, fvalues = inputs
        ckey_float = ckeys.astype(jnp.float32)
        cvalue_float = cvalues.astype(jnp.float32)
        fkey_float = fkeys.astype(jnp.float32)
        fvalue_float = fvalues.astype(jnp.float32)

        def per_block(block_inputs):
            block_queries, block_index = block_inputs
            query_float = block_queries.astype(jnp.float32)
            scale = HEAD_DIM ** (-0.5)
            cscores = jnp.einsum('tgd,skd->tgsk', query_float, ckey_float) * scale
            clive = cache_live[None, None, :, :]
            cscores = jnp.where(clive, cscores, masked_score)
            chigh = lax.optimization_barrier(jnp.max(cscores, -1))
            cweights = jnp.where(clive, jnp.exp(cscores - chigh[..., None]), 0.0)
            ctotal = lax.optimization_barrier(jnp.sum(cweights, -1))
            crounded = lax.optimization_barrier(cweights.astype(jnp.bfloat16)).astype(jnp.float32)
            cmixed = jnp.einsum('tgsk,skd->tgsd', crounded, cvalue_float)
            cpart = lax.optimization_barrier((cmixed / ctotal[..., None]).astype(jnp.bfloat16)).astype(jnp.float32)
            clse = chigh + jnp.log(ctotal)
            fscores = jnp.einsum('tgd,kd->tgk', query_float, fkey_float) * scale
            query_pos = block_index * TOK_DEV + jnp.arange(TOK_DEV, dtype=jnp.int32)
            flive = (jnp.arange(TOKENS, dtype=jnp.int32)[None, :] <= query_pos[:, None])[:, None, :]
            fscores = jnp.where(flive, fscores, masked_score)
            fhigh = lax.optimization_barrier(jnp.max(fscores, -1))
            fweights = jnp.where(flive, jnp.exp(fscores - fhigh[..., None]), 0.0)
            ftotal = lax.optimization_barrier(jnp.sum(fweights, -1))
            frounded = lax.optimization_barrier(fweights.astype(jnp.bfloat16)).astype(jnp.float32)
            fmixed = jnp.einsum('tgk,kd->tgd', frounded, fvalue_float)
            top = jnp.maximum(lax.optimization_barrier(jnp.max(clse, -1)), fhigh)
            cscale = jnp.exp(clse - top[..., None])
            fscale = jnp.exp(fhigh - top)
            numer = lax.optimization_barrier(jnp.sum(cpart * cscale[..., None], 2)) + fmixed * fscale[..., None]
            denom = lax.optimization_barrier(jnp.sum(cscale, -1)) + ftotal * fscale
            return numer / denom[..., None]
        return lax.map(per_block, (head_queries, jnp.arange(SHARDS, dtype=jnp.int32)))
    outputs = lax.map(per_head, (grouped, cache_key_heads, cache_value_heads, fresh_key_heads, fresh_value_heads))
    return outputs.transpose(1, 2, 0, 3, 4).reshape(TOKENS, HEADS * HEAD_DIM).astype(jnp.bfloat16)
```

```python
import functools

import jax
import jax.numpy as jnp
from jax import lax
from jax.experimental import pallas as pl
from jax.experimental.pallas import tpu as pltpu
from jax.sharding import PartitionSpec as P

HEAD_DIM = 128
MESH = pl.DeviceIdType.MESH

epsilon = 1e-05
rope_base = 500000.0
masked_score = -1e30
score_scale = HEAD_DIM ** (-0.5)
log2e = 1.4426950408889634


def project_kernel(
    n, heads, tok_hbm, gain_ref, wq_hbm, wk_hbm, wv_hbm, ck_hbm, cv_hbm, cos_ref, sin_ref,
    q_out, k_out, v_out, fk_out, fv_out,
    wq, wk, wv, toks, normed, fk, fv,
    w_sem, own_sem, tok_send, tok_recv, c_send, c_recv, f_send, f_recv,
):
    me = lax.axis_index("ctx")
    h = lax.axis_index("head")
    chips = n // 2
    chip = me // 2
    core = me % 2
    sibling = chip * 2 + 1 - core
    width = toks.shape[2]

    weights = [
        pltpu.make_async_copy(src, dst, w_sem.at[i])
        for i, (src, dst) in enumerate(((wk_hbm, wk), (wv_hbm, wv), (wq_hbm, wq)))
    ]

    barrier = pltpu.get_barrier_semaphore()
    for d in range(1, chips):
        pl.semaphore_signal(
            barrier, inc=1, device_id=(((chip + d) % chips) * 2 + core, h), device_id_type=MESH
        )
    pl.semaphore_signal(barrier, inc=1, device_id=(sibling, h), device_id_type=MESH)
    for step in (1, heads - 1):
        pl.semaphore_signal(
            barrier, inc=1, device_id=(me, (h + step) % heads), device_id_type=MESH
        )
    pl.semaphore_wait(barrier, chips + 2)

    def token_copy(way, s):
        origin = h - (s - 1) if way == 0 else h + (s - 1)
        target = h + 1 if way == 0 else h - 1
        src = tok_hbm if s == 1 else toks.at[origin]
        return pltpu.make_async_remote_copy(
            src_ref=src,
            dst_ref=toks.at[origin],
            send_sem=tok_send.at[way, s - 1],
            recv_sem=tok_recv.at[way, s - 1],
            device_id=(me, target),
            device_id_type=MESH,
        )

    def sends(way, s):
        if way == 0:
            return (h >= s - 1) & (h + 1 < heads)
        return (h + s - 1 < heads) & (h >= 1)

    def receives(way, s):
        return h >= s if way == 0 else h + s < heads

    def received(way, s):
        origin = h - s if way == 0 else h + s
        return pltpu.make_async_remote_copy(
            src_ref=toks.at[origin],
            dst_ref=toks.at[origin],
            send_sem=tok_send.at[way, s - 1],
            recv_sem=tok_recv.at[way, s - 1],
            device_id=(me, (h + 1) % heads),
            device_id_type=MESH,
        )

    def block_copy(array, src, out, origin, target, sends_, recvs_, d):
        return pltpu.make_async_remote_copy(
            src_ref=src,
            dst_ref=out.at[origin],
            send_sem=sends_.at[array, d],
            recv_sem=recvs_.at[array, d],
            device_id=(target, h),
            device_id_type=MESH,
        )

    def spread(array, src, out):
        copies = []
        for d in range(1, chips):
            target = ((chip + d) % chips) * 2 + core
            copies.append(block_copy(array, src, out, me, target, c_send, c_recv, d))
        copies.append(block_copy(array, src, out, me, sibling, c_send, c_recv, 0))
        for copy in copies:
            copy.start()
        own = pltpu.make_async_copy(src, out.at[me], own_sem.at[array])
        own.start()
        return copies, own

    for way in (0, 1):
        @pl.when(sends(way, 1))
        def _():
            token_copy(way, 1).start()
    own_tok = pltpu.make_async_copy(tok_hbm, toks.at[h], own_sem.at[4])
    own_tok.start()
    pending = [spread(0, ck_hbm, k_out), spread(1, cv_hbm, v_out)]
    for copy in weights:
        copy.start()

    for s in range(1, heads):
        for way in (0, 1):
            @pl.when(receives(way, s))
            def _():
                received(way, s).wait_recv()
            if s + 1 < heads:
                @pl.when(sends(way, s + 1))
                def _():
                    token_copy(way, s + 1).start()
    own_tok.wait()

    square = jnp.zeros((toks.shape[1], 1), jnp.float32)
    for o in range(heads):
        part = toks[o].astype(jnp.float32)
        square += jnp.sum(part * part, -1, keepdims=True)
    inverse = lax.rsqrt(square / (heads * width) + epsilon)
    for o in range(heads):
        cols = slice(o * width, (o + 1) * width)
        part = toks[o].astype(jnp.float32)
        normed[:, cols] = (part * inverse * gain_ref[:, cols]).astype(jnp.bfloat16)

    def rotated(u):
        return (u * cos_ref[...] + pltpu.roll(u, HEAD_DIM // 2, 1) * sin_ref[...]).astype(
            jnp.bfloat16
        )

    weights[0].wait()
    keys = jnp.dot(normed[...], wk[...], preferred_element_type=jnp.float32)
    for j in range(wk.shape[1] // HEAD_DIM):
        cols = slice(j * HEAD_DIM, (j + 1) * HEAD_DIM)
        fk[:, cols] = rotated(keys[:, cols])
    weights[1].wait()
    fv[...] = jnp.dot(normed[...], wv[...], preferred_element_type=jnp.float32).astype(
        jnp.bfloat16
    )
    pending += [spread(2, fk, fk_out), spread(3, fv, fv_out)]
    weights[2].wait()
    tile = 2 * HEAD_DIM

    @pl.loop(0, wq.shape[1] // tile)
    def _(t):
        cols = pl.ds(pl.multiple_of(t * tile, tile), tile)
        found = jnp.dot(normed[...], wq[:, cols], preferred_element_type=jnp.float32)
        for j in range(2):
            q_out[2 * t + j] = rotated(found[:, j * HEAD_DIM : (j + 1) * HEAD_DIM])

    forwards = []
    for d in range(1, chips):
        for array, out in ((0, k_out), (1, v_out), (2, fk_out), (3, fv_out)):
            origin = ((chip + chips - d) % chips) * 2 + core
            block_copy(array, out.at[origin], out, origin, sibling, c_send, c_recv, d).wait_recv()
            copy = block_copy(array, out.at[origin], out, origin, sibling, f_send, f_recv, d)
            copy.start()
            forwards.append(copy)
    for array, out in ((0, k_out), (1, v_out), (2, fk_out), (3, fv_out)):
        block_copy(array, out.at[sibling], out, sibling, sibling, c_send, c_recv, 0).wait_recv()
        for d in range(1, chips):
            origin = ((chip + chips - d) % chips) * 2 + 1 - core
            block_copy(array, out.at[origin], out, origin, sibling, f_send, f_recv, d).wait_recv()
    for copy in forwards:
        copy.wait_send()
    for copies, own in pending:
        own.wait()
        for copy in copies:
            copy.wait_send()
    for s in range(1, heads):
        for way in (0, 1):
            @pl.when(sends(way, s))
            def _():
                token_copy(way, s).wait_send()


def attend_kernel(n, scalars, q_ref, k_ref, v_ref, fk_ref, fv_ref, out_ref, num, den, top):
    c = pl.program_id(1)
    group, tok_rows = q_ref.shape[0], q_ref.shape[1]
    cache_rows = k_ref.shape[1]
    fresh_rows = fk_ref.shape[0]

    def weigh(q, keys, values, bias):
        scores = lax.dot_general(
            q, keys, (((1,), (1,)), ((), ())), preferred_element_type=jnp.float32
        )
        scores = scores + bias
        high = jnp.max(scores, -1, keepdims=True)
        weights = jnp.exp2((scores - high) * (score_scale * log2e))
        total = jnp.sum(weights, -1, keepdims=True)
        mixed = jnp.dot(
            weights.astype(jnp.bfloat16), values, preferred_element_type=jnp.float32
        )
        return mixed, high * score_scale, total

    @pl.when(c == 0)
    def _():
        num[...] = jnp.zeros_like(num)
        den[...] = jnp.zeros_like(den)
        top[...] = jnp.full_like(top, masked_score)

    length = scalars[jnp.minimum(c, n - 1)]
    pieces = 4
    pair = 2 if group % 2 == 0 else 1

    def cache_step(live):
        bias = jnp.where(
            lax.broadcasted_iota(jnp.int32, (1, live), 1) < length, 0.0, masked_score
        ).astype(jnp.float32)
        for i in range(group // pair):
            rows = slice(i * pair * tok_rows, (i + 1) * pair * tok_rows)
            q = q_ref[i * pair : (i + 1) * pair].reshape(pair * tok_rows, HEAD_DIM)
            mixed, high, total = weigh(q, k_ref[0, :live], v_ref[0, :live], bias)
            part = (mixed / total).astype(jnp.bfloat16).astype(jnp.float32)
            lse = high + jnp.log(total)
            before = top[rows]
            now = jnp.maximum(before, lse)
            keep = jnp.exp(before - now)
            add = jnp.exp(lse - now)
            num[rows] = num[rows] * keep + part * add
            den[rows] = den[rows] * keep + add
            top[rows] = now

    def fresh_step(live):
        first = scalars[n] * tok_rows
        seen = lax.broadcasted_iota(jnp.int32, (tok_rows, live), 1) <= (
            first + lax.broadcasted_iota(jnp.int32, (tok_rows, live), 0)
        )
        bias = jnp.where(seen, 0.0, masked_score).astype(jnp.float32)
        for i in range(group):
            rows = slice(i * tok_rows, (i + 1) * tok_rows)
            mixed, high, total = weigh(q_ref[i], fk_ref[:live], fv_ref[:live], bias)
            before = top[rows]
            now = jnp.maximum(before, high)
            keep = jnp.exp(before - now)
            add = jnp.exp(high - now)
            value = (num[rows] * keep + mixed * add) / (den[rows] * keep + total * add)
            out_ref[:, i * HEAD_DIM : (i + 1) * HEAD_DIM] = value.astype(jnp.bfloat16)

    step = cache_rows // pieces
    fresh_step_rows = fresh_rows // pieces
    fresh_length = (scalars[n] + 1) * tok_rows
    for piece in range(pieces):
        @pl.when((c < n) & (length > piece * step) & (length <= (piece + 1) * step))
        def _():
            cache_step((piece + 1) * step)

        @pl.when(
            (c == n)
            & (fresh_length > piece * fresh_step_rows)
            & (fresh_length <= (piece + 1) * fresh_step_rows)
        )
        def _():
            fresh_step((piece + 1) * fresh_step_rows)


def body(
    tokens, norm_gain, query_weight, key_weight, value_weight, cache_keys, cache_values,
    cache_lengths, start_position,
):
    n = lax.axis_size("ctx")
    heads = lax.axis_size("head")
    rank = lax.axis_index("ctx")
    tok_rows, width = tokens.shape
    model = query_weight.shape[0]
    kv_cols = key_weight.shape[1]
    q_cols = query_weight.shape[1]
    cache_rows = cache_keys.shape[0]
    local_kv = kv_cols // HEAD_DIM
    local_q = q_cols // HEAD_DIM
    group = local_q // local_kv
    half = HEAD_DIM // 2
    position = (start_position[0] + rank * tok_rows + jnp.arange(tok_rows, dtype=jnp.int32)).astype(
        jnp.float32
    )
    freqs = jnp.power(
        jnp.float32(rope_base), -2.0 * jnp.arange(half, dtype=jnp.float32) / HEAD_DIM
    )
    angles = position[:, None] * freqs[None, :]
    cosine, sine = jnp.cos(angles), jnp.sin(angles)
    cos_table = jnp.concatenate([cosine, cosine], -1)
    sin_table = jnp.concatenate([-sine, sine], -1)

    anywhere = pl.BlockSpec(memory_space=pl.ANY)
    vmem = pl.BlockSpec(memory_space=pltpu.VMEM)
    bf16 = jnp.bfloat16
    chips = n // 2
    q, all_k, all_v, fresh_k, fresh_v = pl.pallas_call(
        functools.partial(project_kernel, n, heads),
        out_shape=[
            jax.ShapeDtypeStruct((local_q, tok_rows, HEAD_DIM), bf16),
            jax.ShapeDtypeStruct((n, cache_rows, kv_cols), bf16),
            jax.ShapeDtypeStruct((n, cache_rows, kv_cols), bf16),
            jax.ShapeDtypeStruct((n, tok_rows, kv_cols), bf16),
            jax.ShapeDtypeStruct((n, tok_rows, kv_cols), bf16),
        ],
        in_specs=[anywhere, vmem, anywhere, anywhere, anywhere, anywhere, anywhere, vmem, vmem],
        out_specs=[vmem, anywhere, anywhere, anywhere, anywhere],
        scratch_shapes=[
            pltpu.VMEM((model, q_cols), bf16),
            pltpu.VMEM((model, kv_cols), bf16),
            pltpu.VMEM((model, kv_cols), bf16),
            pltpu.VMEM((heads, tok_rows, width), bf16),
            pltpu.VMEM((tok_rows, model), bf16),
            pltpu.VMEM((tok_rows, kv_cols), bf16),
            pltpu.VMEM((tok_rows, kv_cols), bf16),
            pltpu.SemaphoreType.DMA((3,)),
            pltpu.SemaphoreType.DMA((5,)),
            pltpu.SemaphoreType.DMA((2, heads)),
            pltpu.SemaphoreType.DMA((2, heads)),
            pltpu.SemaphoreType.DMA((4, chips)),
            pltpu.SemaphoreType.DMA((4, chips)),
            pltpu.SemaphoreType.DMA((4, chips)),
            pltpu.SemaphoreType.DMA((4, chips)),
        ],
        compiler_params=pltpu.CompilerParams(
            collective_id=0, has_side_effects=True, vmem_limit_bytes=56 * 2**20
        ),
        name="gather_project",
    )(
        tokens, norm_gain[None, :], query_weight, key_weight, value_weight, cache_keys,
        cache_values, cos_table, sin_table,
    )

    fresh_k = fresh_k.reshape(n * tok_rows, kv_cols)
    fresh_v = fresh_v.reshape(n * tok_rows, kv_cols)
    scalars = jnp.concatenate([cache_lengths, rank.astype(jnp.int32)[None]])
    cache_spec = pl.BlockSpec(
        (1, cache_rows, HEAD_DIM), lambda g, c, s: (jnp.minimum(c, n - 1), 0, g)
    )
    fresh_spec = pl.BlockSpec((n * tok_rows, HEAD_DIM), lambda g, c, s: (0, g))
    rows = group * tok_rows
    return pl.pallas_call(
        functools.partial(attend_kernel, n),
        out_shape=jax.ShapeDtypeStruct((tok_rows, q_cols), bf16),
        grid_spec=pltpu.PrefetchScalarGridSpec(
            num_scalar_prefetch=1,
            grid=(local_kv, n + 1),
            in_specs=[
                pl.BlockSpec((group, tok_rows, HEAD_DIM), lambda g, c, s: (g, 0, 0)),
                cache_spec,
                cache_spec,
                fresh_spec,
                fresh_spec,
            ],
            out_specs=pl.BlockSpec((tok_rows, group * HEAD_DIM), lambda g, c, s: (0, g)),
            scratch_shapes=[
                pltpu.VMEM((rows, HEAD_DIM), jnp.float32),
                pltpu.VMEM((rows, 1), jnp.float32),
                pltpu.VMEM((rows, 1), jnp.float32),
            ],
        ),
        compiler_params=pltpu.CompilerParams(vmem_limit_bytes=48 * 2**20),
        name="attend",
    )(scalars, q, all_k, all_v, fresh_k, fresh_v)


def solution(mesh):
    in_specs = (
        P("ctx", "head"),
        P(),
        P(None, "head"),
        P(None, "head"),
        P(None, "head"),
        P("ctx", "head"),
        P("ctx", "head"),
        P(),
        P(),
    )
    out_specs = P("ctx", "head")
    return jax.shard_map(body, mesh=mesh, in_specs=in_specs, out_specs=out_specs, check_vma=False)
```

```python
import functools

import jax
import jax.numpy as jnp
from jax import lax
from jax.experimental import pallas as pl
from jax.experimental.pallas import tpu as pltpu
from jax.sharding import PartitionSpec as P

HEAD_DIM = 128
MESH = pl.DeviceIdType.MESH

epsilon = 1e-05
rope_base = 500000.0
masked_score = -1e30
score_scale = HEAD_DIM ** (-0.5)
log2e = 1.4426950408889634


def project_kernel(
    n, heads, tok_hbm, gain_ref, wq_hbm, wk_hbm, wv_hbm, ck_hbm, cv_hbm, cos_ref, sin_ref,
    q_out, k_out, v_out, fk_out, fv_out,
    wq, wk, wv, toks, normed, fk, fv,
    w_sem, own_sem, tok_send, tok_recv, c_send, c_recv, f_send, f_recv,
):
    me = lax.axis_index("ctx")
    h = lax.axis_index("head")
    chips = n // 2
    chip = me // 2
    core = me % 2
    sibling = chip * 2 + 1 - core
    width = toks.shape[2]
    square_plane = chips == 4
    across, along = chip // 2, chip % 2
    near = (None, across * 2 + 1 - along, (1 - across) * 2 + along, 3 - chip)

    def to_peer(d):
        found = near[d] if square_plane else (chip + d) % chips
        return found * 2 + core

    def from_chip(d):
        return near[d] if square_plane else (chip + chips - d) % chips

    weights = [
        pltpu.make_async_copy(src, dst, w_sem.at[i])
        for i, (src, dst) in enumerate(((wk_hbm, wk), (wv_hbm, wv), (wq_hbm, wq)))
    ]

    barrier = pltpu.get_barrier_semaphore()
    for d in range(1, chips):
        pl.semaphore_signal(
            barrier, inc=1, device_id=(to_peer(d), h), device_id_type=MESH
        )
    pl.semaphore_signal(barrier, inc=1, device_id=(sibling, h), device_id_type=MESH)
    for step in (1, heads - 1):
        pl.semaphore_signal(
            barrier, inc=1, device_id=(me, (h + step) % heads), device_id_type=MESH
        )
    pl.semaphore_wait(barrier, chips + 2)

    def token_copy(way, s):
        origin = h - (s - 1) if way == 0 else h + (s - 1)
        target = h + 1 if way == 0 else h - 1
        src = tok_hbm if s == 1 else toks.at[origin]
        return pltpu.make_async_remote_copy(
            src_ref=src,
            dst_ref=toks.at[origin],
            send_sem=tok_send.at[way, s - 1],
            recv_sem=tok_recv.at[way, s - 1],
            device_id=(me, target),
            device_id_type=MESH,
        )

    def sends(way, s):
        if way == 0:
            return (h >= s - 1) & (h + 1 < heads)
        return (h + s - 1 < heads) & (h >= 1)

    def receives(way, s):
        return h >= s if way == 0 else h + s < heads

    def received(way, s):
        origin = h - s if way == 0 else h + s
        return pltpu.make_async_remote_copy(
            src_ref=toks.at[origin],
            dst_ref=toks.at[origin],
            send_sem=tok_send.at[way, s - 1],
            recv_sem=tok_recv.at[way, s - 1],
            device_id=(me, (h + 1) % heads),
            device_id_type=MESH,
        )

    def block_copy(array, src, out, origin, target, sends_, recvs_, d):
        return pltpu.make_async_remote_copy(
            src_ref=src,
            dst_ref=out.at[origin],
            send_sem=sends_.at[array, d],
            recv_sem=recvs_.at[array, d],
            device_id=(target, h),
            device_id_type=MESH,
        )

    def spread(array, src, out, direct):
        copies = []
        for d in range(1, direct):
            copies.append(block_copy(array, src, out, me, to_peer(d), c_send, c_recv, d))
        copies.append(block_copy(array, src, out, me, sibling, c_send, c_recv, 0))
        for copy in copies:
            copy.start()
        own = pltpu.make_async_copy(src, out.at[me], own_sem.at[array])
        own.start()
        return copies, own

    for way in (0, 1):
        @pl.when(sends(way, 1))
        def _():
            token_copy(way, 1).start()
    own_tok = pltpu.make_async_copy(tok_hbm, toks.at[h], own_sem.at[4])
    own_tok.start()
    direct = 3 if square_plane else chips
    pending = [spread(0, ck_hbm, k_out, direct), spread(1, cv_hbm, v_out, direct)]
    outs = (k_out, v_out, fk_out, fv_out)
    forwards = []

    def arrived(array, d):
        origin = from_chip(d) * 2 + core
        out = outs[array]
        block_copy(array, out.at[origin], out, origin, sibling, c_send, c_recv, d).wait_recv()
        return out.at[origin], out, origin

    def forward(array, d):
        src, out, origin = arrived(array, d)
        hand_on(array, src, out, origin, d)

    def hand_on(array, src, out, origin, d):
        copy = block_copy(array, src, out, origin, sibling, f_send, f_recv, d)
        copy.start()
        forwards.append(copy)

    def relay(array, source, target):
        src, out, origin = arrived(array, source)
        copy = block_copy(array, src, out, origin, to_peer(target), c_send, c_recv, 3)
        copy.start()
        forwards.append(copy)
        hand_on(array, src, out, origin, source)

    for copy in weights:
        copy.start()

    for s in range(1, heads):
        for way in (0, 1):
            @pl.when(receives(way, s))
            def _():
                received(way, s).wait_recv()
            if s + 1 < heads:
                @pl.when(sends(way, s + 1))
                def _():
                    token_copy(way, s + 1).start()
        if square_plane and s == max(1, heads - 2):
            relay(0, 1, 2)
            relay(1, 2, 1)
    if square_plane:
        forward(0, 2)
        forward(1, 1)
    own_tok.wait()

    square = jnp.zeros((toks.shape[1], 1), jnp.float32)
    for o in range(heads):
        part = toks[o].astype(jnp.float32)
        square += jnp.sum(part * part, -1, keepdims=True)
    inverse = lax.rsqrt(square / (heads * width) + epsilon)
    for o in range(heads):
        cols = slice(o * width, (o + 1) * width)
        part = toks[o].astype(jnp.float32)
        normed[:, cols] = (part * inverse * gain_ref[:, cols]).astype(jnp.bfloat16)

    def rotated(u):
        return (u * cos_ref[...] + pltpu.roll(u, HEAD_DIM // 2, 1) * sin_ref[...]).astype(
            jnp.bfloat16
        )

    weights[0].wait()
    keys = jnp.dot(normed[...], wk[...], preferred_element_type=jnp.float32)
    for j in range(wk.shape[1] // HEAD_DIM):
        cols = slice(j * HEAD_DIM, (j + 1) * HEAD_DIM)
        fk[:, cols] = rotated(keys[:, cols])
    weights[1].wait()
    fv[...] = jnp.dot(normed[...], wv[...], preferred_element_type=jnp.float32).astype(
        jnp.bfloat16
    )
    pending += [spread(2, fk, fk_out, chips), spread(3, fv, fv_out, chips)]
    weights[2].wait()
    tile = 2 * HEAD_DIM

    @pl.loop(0, wq.shape[1] // tile)
    def _(t):
        cols = pl.ds(pl.multiple_of(t * tile, tile), tile)
        found = jnp.dot(normed[...], wq[:, cols], preferred_element_type=jnp.float32)
        for j in range(2):
            q_out[2 * t + j] = rotated(found[:, j * HEAD_DIM : (j + 1) * HEAD_DIM])

    for d in (3,) if square_plane else range(1, chips):
        forward(0, d)
        forward(1, d)
    for d in range(1, chips):
        forward(2, d)
        forward(3, d)
    for array, out in enumerate(outs):
        block_copy(array, out.at[sibling], out, sibling, sibling, c_send, c_recv, 0).wait_recv()
        for d in range(1, chips):
            origin = from_chip(d) * 2 + 1 - core
            block_copy(array, out.at[origin], out, origin, sibling, f_send, f_recv, d).wait_recv()
    for copy in forwards:
        copy.wait_send()
    for copies, own in pending:
        own.wait()
        for copy in copies:
            copy.wait_send()
    for s in range(1, heads):
        for way in (0, 1):
            @pl.when(sends(way, s))
            def _():
                token_copy(way, s).wait_send()


def attend_kernel(n, scalars, q_ref, k_ref, v_ref, fk_ref, fv_ref, out_ref, num, den, top):
    c = pl.program_id(1)
    group, tok_rows = q_ref.shape[0], q_ref.shape[1]
    cache_rows = k_ref.shape[1]
    fresh_rows = fk_ref.shape[0]

    def weigh(q, keys, values, bias):
        scores = lax.dot_general(
            q, keys, (((1,), (1,)), ((), ())), preferred_element_type=jnp.float32
        )
        scores = scores + bias
        high = jnp.max(scores, -1, keepdims=True)
        weights = jnp.exp2((scores - high) * (score_scale * log2e))
        total = jnp.sum(weights, -1, keepdims=True)
        mixed = jnp.dot(
            weights.astype(jnp.bfloat16), values, preferred_element_type=jnp.float32
        )
        return mixed, high * score_scale, total

    @pl.when(c == 0)
    def _():
        num[...] = jnp.zeros_like(num)
        den[...] = jnp.zeros_like(den)
        top[...] = jnp.full_like(top, masked_score)

    length = scalars[jnp.minimum(c, n - 1)]
    pieces = 4
    pair = 2 if group % 2 == 0 else 1

    def cache_step(live):
        bias = jnp.where(
            lax.broadcasted_iota(jnp.int32, (1, live), 1) < length, 0.0, masked_score
        ).astype(jnp.float32)
        for i in range(group // pair):
            rows = slice(i * pair * tok_rows, (i + 1) * pair * tok_rows)
            q = q_ref[i * pair : (i + 1) * pair].reshape(pair * tok_rows, HEAD_DIM)
            mixed, high, total = weigh(q, k_ref[0, :live], v_ref[0, :live], bias)
            part = (mixed / total).astype(jnp.bfloat16).astype(jnp.float32)
            lse = high + jnp.log(total)
            before = top[rows]
            now = jnp.maximum(before, lse)
            keep = jnp.exp(before - now)
            add = jnp.exp(lse - now)
            num[rows] = num[rows] * keep + part * add
            den[rows] = den[rows] * keep + add
            top[rows] = now

    def fresh_step(live):
        first = scalars[n] * tok_rows
        seen = lax.broadcasted_iota(jnp.int32, (tok_rows, live), 1) <= (
            first + lax.broadcasted_iota(jnp.int32, (tok_rows, live), 0)
        )
        bias = jnp.where(seen, 0.0, masked_score).astype(jnp.float32)
        for i in range(group):
            rows = slice(i * tok_rows, (i + 1) * tok_rows)
            mixed, high, total = weigh(q_ref[i], fk_ref[:live], fv_ref[:live], bias)
            before = top[rows]
            now = jnp.maximum(before, high)
            keep = jnp.exp(before - now)
            add = jnp.exp(high - now)
            value = (num[rows] * keep + mixed * add) / (den[rows] * keep + total * add)
            out_ref[:, i * HEAD_DIM : (i + 1) * HEAD_DIM] = value.astype(jnp.bfloat16)

    step = cache_rows // pieces
    fresh_step_rows = fresh_rows // pieces
    fresh_length = (scalars[n] + 1) * tok_rows
    for piece in range(pieces):
        @pl.when((c < n) & (length > piece * step) & (length <= (piece + 1) * step))
        def _():
            cache_step((piece + 1) * step)

        @pl.when(
            (c == n)
            & (fresh_length > piece * fresh_step_rows)
            & (fresh_length <= (piece + 1) * fresh_step_rows)
        )
        def _():
            fresh_step((piece + 1) * fresh_step_rows)


def body(
    tokens, norm_gain, query_weight, key_weight, value_weight, cache_keys, cache_values,
    cache_lengths, start_position,
):
    n = lax.axis_size("ctx")
    heads = lax.axis_size("head")
    rank = lax.axis_index("ctx")
    tok_rows, width = tokens.shape
    model = query_weight.shape[0]
    kv_cols = key_weight.shape[1]
    q_cols = query_weight.shape[1]
    cache_rows = cache_keys.shape[0]
    local_kv = kv_cols // HEAD_DIM
    local_q = q_cols // HEAD_DIM
    group = local_q // local_kv
    half = HEAD_DIM // 2
    position = (start_position[0] + rank * tok_rows + jnp.arange(tok_rows, dtype=jnp.int32)).astype(
        jnp.float32
    )
    freqs = jnp.power(
        jnp.float32(rope_base), -2.0 * jnp.arange(half, dtype=jnp.float32) / HEAD_DIM
    )
    angles = position[:, None] * freqs[None, :]
    cosine, sine = jnp.cos(angles), jnp.sin(angles)
    cos_table = jnp.concatenate([cosine, cosine], -1)
    sin_table = jnp.concatenate([-sine, sine], -1)

    anywhere = pl.BlockSpec(memory_space=pl.ANY)
    vmem = pl.BlockSpec(memory_space=pltpu.VMEM)
    bf16 = jnp.bfloat16
    chips = n // 2
    q, all_k, all_v, fresh_k, fresh_v = pl.pallas_call(
        functools.partial(project_kernel, n, heads),
        out_shape=[
            jax.ShapeDtypeStruct((local_q, tok_rows, HEAD_DIM), bf16),
            jax.ShapeDtypeStruct((n, cache_rows, kv_cols), bf16),
            jax.ShapeDtypeStruct((n, cache_rows, kv_cols), bf16),
            jax.ShapeDtypeStruct((n, tok_rows, kv_cols), bf16),
            jax.ShapeDtypeStruct((n, tok_rows, kv_cols), bf16),
        ],
        in_specs=[anywhere, vmem, anywhere, anywhere, anywhere, anywhere, anywhere, vmem, vmem],
        out_specs=[vmem, anywhere, anywhere, anywhere, anywhere],
        scratch_shapes=[
            pltpu.VMEM((model, q_cols), bf16),
            pltpu.VMEM((model, kv_cols), bf16),
            pltpu.VMEM((model, kv_cols), bf16),
            pltpu.VMEM((heads, tok_rows, width), bf16),
            pltpu.VMEM((tok_rows, model), bf16),
            pltpu.VMEM((tok_rows, kv_cols), bf16),
            pltpu.VMEM((tok_rows, kv_cols), bf16),
            pltpu.SemaphoreType.DMA((3,)),
            pltpu.SemaphoreType.DMA((5,)),
            pltpu.SemaphoreType.DMA((2, heads)),
            pltpu.SemaphoreType.DMA((2, heads)),
            pltpu.SemaphoreType.DMA((4, chips)),
            pltpu.SemaphoreType.DMA((4, chips)),
            pltpu.SemaphoreType.DMA((4, chips)),
            pltpu.SemaphoreType.DMA((4, chips)),
        ],
        compiler_params=pltpu.CompilerParams(
            collective_id=0, has_side_effects=True, vmem_limit_bytes=56 * 2**20
        ),
        name="gather_project",
    )(
        tokens, norm_gain[None, :], query_weight, key_weight, value_weight, cache_keys,
        cache_values, cos_table, sin_table,
    )

    fresh_k = fresh_k.reshape(n * tok_rows, kv_cols)
    fresh_v = fresh_v.reshape(n * tok_rows, kv_cols)
    scalars = jnp.concatenate([cache_lengths, rank.astype(jnp.int32)[None]])
    cache_spec = pl.BlockSpec(
        (1, cache_rows, HEAD_DIM), lambda g, c, s: (jnp.minimum(c, n - 1), 0, g)
    )
    fresh_spec = pl.BlockSpec((n * tok_rows, HEAD_DIM), lambda g, c, s: (0, g))
    rows = group * tok_rows
    return pl.pallas_call(
        functools.partial(attend_kernel, n),
        out_shape=jax.ShapeDtypeStruct((tok_rows, q_cols), bf16),
        grid_spec=pltpu.PrefetchScalarGridSpec(
            num_scalar_prefetch=1,
            grid=(local_kv, n + 1),
            in_specs=[
                pl.BlockSpec((group, tok_rows, HEAD_DIM), lambda g, c, s: (g, 0, 0)),
                cache_spec,
                cache_spec,
                fresh_spec,
                fresh_spec,
            ],
            out_specs=pl.BlockSpec((tok_rows, group * HEAD_DIM), lambda g, c, s: (0, g)),
            scratch_shapes=[
                pltpu.VMEM((rows, HEAD_DIM), jnp.float32),
                pltpu.VMEM((rows, 1), jnp.float32),
                pltpu.VMEM((rows, 1), jnp.float32),
            ],
        ),
        compiler_params=pltpu.CompilerParams(vmem_limit_bytes=48 * 2**20),
        name="attend",
    )(scalars, q, all_k, all_v, fresh_k, fresh_v)


def solution(mesh):
    in_specs = (
        P("ctx", "head"),
        P(),
        P(None, "head"),
        P(None, "head"),
        P(None, "head"),
        P("ctx", "head"),
        P("ctx", "head"),
        P(),
        P(),
    )
    out_specs = P("ctx", "head")
    return jax.shard_map(body, mesh=mesh, in_specs=in_specs, out_specs=out_specs, check_vma=False)
```

```python
import functools

import jax
import jax.numpy as jnp
from jax import lax
from jax.experimental import pallas as pl
from jax.experimental.pallas import tpu as pltpu
from jax.sharding import PartitionSpec as P

HEAD_DIM = 128
MESH = pl.DeviceIdType.MESH

epsilon = 1e-05
rope_base = 500000.0
masked_score = -1e30
score_scale = HEAD_DIM ** (-0.5)
log2e = 1.4426950408889634


def project_kernel(
    n, heads, tok_hbm, gain_ref, wq_hbm, wk_hbm, wv_hbm, ck_hbm, cv_hbm, cos_ref, sin_ref,
    q_out, k_out, v_out, fk_out, fv_out,
    wq, wk, wv, toks, normed, fk, fv,
    w_sem, own_sem, tok_send, tok_recv, c_send, c_recv, f_send, f_recv,
):
    me = lax.axis_index("ctx")
    h = lax.axis_index("head")
    chips = n // 2
    chip = me // 2
    core = me % 2
    sibling = chip * 2 + 1 - core
    width = toks.shape[2]
    square_plane = chips == 4
    across, along = chip // 2, chip % 2
    near = (None, across * 2 + 1 - along, (1 - across) * 2 + along, 3 - chip)

    def to_peer(d):
        found = near[d] if square_plane else (chip + d) % chips
        return found * 2 + core

    def from_chip(d):
        return near[d] if square_plane else (chip + chips - d) % chips

    weights = [
        pltpu.make_async_copy(src, dst, w_sem.at[i])
        for i, (src, dst) in enumerate(((wk_hbm, wk), (wv_hbm, wv), (wq_hbm, wq)))
    ]

    barrier = pltpu.get_barrier_semaphore()
    for d in range(1, chips):
        pl.semaphore_signal(
            barrier, inc=1, device_id=(to_peer(d), h), device_id_type=MESH
        )
    pl.semaphore_signal(barrier, inc=1, device_id=(sibling, h), device_id_type=MESH)
    for step in (1, heads - 1):
        pl.semaphore_signal(
            barrier, inc=1, device_id=(me, (h + step) % heads), device_id_type=MESH
        )
    pl.semaphore_wait(barrier, chips + 2)

    def token_copy(way, s):
        origin = h - (s - 1) if way == 0 else h + (s - 1)
        target = h + 1 if way == 0 else h - 1
        src = tok_hbm if s == 1 else toks.at[origin]
        return pltpu.make_async_remote_copy(
            src_ref=src,
            dst_ref=toks.at[origin],
            send_sem=tok_send.at[way, s - 1],
            recv_sem=tok_recv.at[way, s - 1],
            device_id=(me, target),
            device_id_type=MESH,
        )

    def sends(way, s):
        if way == 0:
            return (h >= s - 1) & (h + 1 < heads)
        return (h + s - 1 < heads) & (h >= 1)

    def receives(way, s):
        return h >= s if way == 0 else h + s < heads

    def received(way, s):
        origin = h - s if way == 0 else h + s
        return pltpu.make_async_remote_copy(
            src_ref=toks.at[origin],
            dst_ref=toks.at[origin],
            send_sem=tok_send.at[way, s - 1],
            recv_sem=tok_recv.at[way, s - 1],
            device_id=(me, (h + 1) % heads),
            device_id_type=MESH,
        )

    def block_copy(array, src, out, origin, target, sends_, recvs_, d):
        return pltpu.make_async_remote_copy(
            src_ref=src,
            dst_ref=out.at[origin],
            send_sem=sends_.at[array, d],
            recv_sem=recvs_.at[array, d],
            device_id=(target, h),
            device_id_type=MESH,
        )

    def spread(array, src, out, direct):
        copies = []
        for d in range(1, direct):
            copies.append(block_copy(array, src, out, me, to_peer(d), c_send, c_recv, d))
        copies.append(block_copy(array, src, out, me, sibling, c_send, c_recv, 0))
        for copy in copies:
            copy.start()
        own = pltpu.make_async_copy(src, out.at[me], own_sem.at[array])
        own.start()
        return copies, own

    for way in (0, 1):
        @pl.when(sends(way, 1))
        def _():
            token_copy(way, 1).start()
    own_tok = pltpu.make_async_copy(tok_hbm, toks.at[h], own_sem.at[4])
    own_tok.start()
    direct = 3 if square_plane else chips
    pending = [spread(0, ck_hbm, k_out, direct), spread(1, cv_hbm, v_out, direct)]
    outs = (k_out, v_out, fk_out, fv_out)
    forwards = []

    def arrived(array, d):
        origin = from_chip(d) * 2 + core
        out = outs[array]
        block_copy(array, out.at[origin], out, origin, sibling, c_send, c_recv, d).wait_recv()
        return out.at[origin], out, origin

    def forward(array, d):
        src, out, origin = arrived(array, d)
        hand_on(array, src, out, origin, d)

    def hand_on(array, src, out, origin, d):
        copy = block_copy(array, src, out, origin, sibling, f_send, f_recv, d)
        copy.start()
        forwards.append(copy)

    def relay(array, source, target):
        src, out, origin = arrived(array, source)
        copy = block_copy(array, src, out, origin, to_peer(target), c_send, c_recv, 3)
        copy.start()
        forwards.append(copy)
        hand_on(array, src, out, origin, source)

    for copy in weights:
        copy.start()

    for s in range(1, heads):
        for way in (0, 1):
            @pl.when(receives(way, s))
            def _():
                received(way, s).wait_recv()
            if s + 1 < heads:
                @pl.when(sends(way, s + 1))
                def _():
                    token_copy(way, s + 1).start()
        if square_plane and s == max(1, heads - 2):
            relay(0, 1, 2)
            relay(1, 2, 1)
    if square_plane:
        forward(0, 2)
        forward(1, 1)
    own_tok.wait()

    square = jnp.zeros((toks.shape[1], 1), jnp.float32)
    for o in range(heads):
        part = toks[o].astype(jnp.float32)
        square += jnp.sum(part * part, -1, keepdims=True)
    inverse = lax.rsqrt(square / (heads * width) + epsilon)
    for o in range(heads):
        cols = slice(o * width, (o + 1) * width)
        part = toks[o].astype(jnp.float32)
        normed[:, cols] = (part * inverse * gain_ref[:, cols]).astype(jnp.bfloat16)

    def rotated(u):
        return (u * cos_ref[...] + pltpu.roll(u, HEAD_DIM // 2, 1) * sin_ref[...]).astype(
            jnp.bfloat16
        )

    weights[0].wait()
    keys = jnp.dot(normed[...], wk[...], preferred_element_type=jnp.float32)
    for j in range(wk.shape[1] // HEAD_DIM):
        cols = slice(j * HEAD_DIM, (j + 1) * HEAD_DIM)
        fk[:, cols] = rotated(keys[:, cols])
    weights[1].wait()
    fv[...] = jnp.dot(normed[...], wv[...], preferred_element_type=jnp.float32).astype(
        jnp.bfloat16
    )
    pending += [spread(2, fk, fk_out, chips), spread(3, fv, fv_out, chips)]
    weights[2].wait()
    tile = 2 * HEAD_DIM

    @pl.loop(0, wq.shape[1] // tile)
    def _(t):
        cols = pl.ds(pl.multiple_of(t * tile, tile), tile)
        found = jnp.dot(normed[...], wq[:, cols], preferred_element_type=jnp.float32)
        for j in range(2):
            q_out[2 * t + j] = rotated(found[:, j * HEAD_DIM : (j + 1) * HEAD_DIM])

    for d in (3,) if square_plane else range(1, chips):
        forward(0, d)
        forward(1, d)
    for d in range(1, chips):
        forward(2, d)
        forward(3, d)
    for array, out in enumerate(outs):
        block_copy(array, out.at[sibling], out, sibling, sibling, c_send, c_recv, 0).wait_recv()
        for d in range(1, chips):
            origin = from_chip(d) * 2 + 1 - core
            block_copy(array, out.at[origin], out, origin, sibling, f_send, f_recv, d).wait_recv()
    for copy in forwards:
        copy.wait_send()
    for copies, own in pending:
        own.wait()
        for copy in copies:
            copy.wait_send()
    for s in range(1, heads):
        for way in (0, 1):
            @pl.when(sends(way, s))
            def _():
                token_copy(way, s).wait_send()


def attend_kernel(n, scalars, q_ref, k_ref, v_ref, fk_ref, fv_ref, out_ref, num, den, top):
    c = pl.program_id(1)
    group, tok_rows = q_ref.shape[0], q_ref.shape[1]
    cache_rows = k_ref.shape[1]
    fresh_rows = fk_ref.shape[0]

    def weigh(q, keys, values, bias):
        scores = lax.dot_general(
            keys, q, (((1,), (1,)), ((), ())), preferred_element_type=jnp.float32
        )
        clear = scores.shape[0] - bias.shape[0]
        if clear:
            scores = jnp.concatenate([scores[:clear], scores[clear:] + bias], 0)
        else:
            scores = scores + bias
        high = jnp.max(scores, 0, keepdims=True)
        weights = jnp.exp2((scores - high) * (score_scale * log2e))
        total = jnp.sum(weights, 0, keepdims=True)
        mixed = lax.dot_general(
            values, weights.astype(jnp.bfloat16), (((0,), (0,)), ((), ())),
            preferred_element_type=jnp.float32,
        )
        return mixed, high * score_scale, total

    @pl.when(c == 0)
    def _():
        num[...] = jnp.zeros_like(num)
        den[...] = jnp.zeros_like(den)
        top[...] = jnp.full_like(top, masked_score)

    length = scalars[jnp.minimum(c, n - 1)]
    pieces = 4
    pair = group

    def cache_step(live):
        bias = jnp.where(
            lax.broadcasted_iota(jnp.int32, (step, pair * tok_rows), 0) < length - (live - step),
            0.0,
            masked_score,
        ).astype(jnp.float32)
        for i in range(group // pair):
            rows = slice(i * pair * tok_rows, (i + 1) * pair * tok_rows)
            q = q_ref[i * pair : (i + 1) * pair].reshape(pair * tok_rows, HEAD_DIM)
            mixed, high, total = weigh(q, k_ref[0, :live], v_ref[0, :live], bias)
            part = (mixed / total).astype(jnp.bfloat16).astype(jnp.float32)
            lse = high + jnp.log(total)
            before = top[:, rows]
            now = jnp.maximum(before, lse)
            keep = jnp.exp(before - now)
            add = jnp.exp(lse - now)
            num[:, rows] = num[:, rows] * keep + part * add
            den[:, rows] = den[:, rows] * keep + add
            top[:, rows] = now

    def fresh_step(live):
        first = scalars[n] * tok_rows
        seen = lax.broadcasted_iota(jnp.int32, (live, tok_rows), 0) <= (
            first + lax.broadcasted_iota(jnp.int32, (live, tok_rows), 1)
        )
        bias = jnp.where(seen, 0.0, masked_score).astype(jnp.float32)
        for i in range(group):
            rows = slice(i * tok_rows, (i + 1) * tok_rows)
            mixed, high, total = weigh(q_ref[i], fk_ref[:live], fv_ref[:live], bias)
            before = top[:, rows]
            now = jnp.maximum(before, high)
            keep = jnp.exp(before - now)
            add = jnp.exp(high - now)
            value = (num[:, rows] * keep + mixed * add) / (den[:, rows] * keep + total * add)
            out_ref[:, i * HEAD_DIM : (i + 1) * HEAD_DIM] = value.T.astype(jnp.bfloat16)

    step = cache_rows // pieces
    fresh_step_rows = fresh_rows // pieces
    fresh_length = (scalars[n] + 1) * tok_rows
    for piece in range(pieces):
        @pl.when((c < n) & (length > piece * step) & (length <= (piece + 1) * step))
        def _():
            cache_step((piece + 1) * step)

        @pl.when(
            (c == n)
            & (fresh_length > piece * fresh_step_rows)
            & (fresh_length <= (piece + 1) * fresh_step_rows)
        )
        def _():
            fresh_step((piece + 1) * fresh_step_rows)


def body(
    tokens, norm_gain, query_weight, key_weight, value_weight, cache_keys, cache_values,
    cache_lengths, start_position,
):
    n = lax.axis_size("ctx")
    heads = lax.axis_size("head")
    rank = lax.axis_index("ctx")
    tok_rows, width = tokens.shape
    model = query_weight.shape[0]
    kv_cols = key_weight.shape[1]
    q_cols = query_weight.shape[1]
    cache_rows = cache_keys.shape[0]
    local_kv = kv_cols // HEAD_DIM
    local_q = q_cols // HEAD_DIM
    group = local_q // local_kv
    half = HEAD_DIM // 2
    position = (start_position[0] + rank * tok_rows + jnp.arange(tok_rows, dtype=jnp.int32)).astype(
        jnp.float32
    )
    freqs = jnp.power(
        jnp.float32(rope_base), -2.0 * jnp.arange(half, dtype=jnp.float32) / HEAD_DIM
    )
    angles = position[:, None] * freqs[None, :]
    cosine, sine = jnp.cos(angles), jnp.sin(angles)
    cos_table = jnp.concatenate([cosine, cosine], -1)
    sin_table = jnp.concatenate([-sine, sine], -1)

    anywhere = pl.BlockSpec(memory_space=pl.ANY)
    vmem = pl.BlockSpec(memory_space=pltpu.VMEM)
    bf16 = jnp.bfloat16
    chips = n // 2
    q, all_k, all_v, fresh_k, fresh_v = pl.pallas_call(
        functools.partial(project_kernel, n, heads),
        out_shape=[
            jax.ShapeDtypeStruct((local_q, tok_rows, HEAD_DIM), bf16),
            jax.ShapeDtypeStruct((n, cache_rows, kv_cols), bf16),
            jax.ShapeDtypeStruct((n, cache_rows, kv_cols), bf16),
            jax.ShapeDtypeStruct((n, tok_rows, kv_cols), bf16),
            jax.ShapeDtypeStruct((n, tok_rows, kv_cols), bf16),
        ],
        in_specs=[anywhere, vmem, anywhere, anywhere, anywhere, anywhere, anywhere, vmem, vmem],
        out_specs=[vmem, anywhere, anywhere, anywhere, anywhere],
        scratch_shapes=[
            pltpu.VMEM((model, q_cols), bf16),
            pltpu.VMEM((model, kv_cols), bf16),
            pltpu.VMEM((model, kv_cols), bf16),
            pltpu.VMEM((heads, tok_rows, width), bf16),
            pltpu.VMEM((tok_rows, model), bf16),
            pltpu.VMEM((tok_rows, kv_cols), bf16),
            pltpu.VMEM((tok_rows, kv_cols), bf16),
            pltpu.SemaphoreType.DMA((3,)),
            pltpu.SemaphoreType.DMA((5,)),
            pltpu.SemaphoreType.DMA((2, heads)),
            pltpu.SemaphoreType.DMA((2, heads)),
            pltpu.SemaphoreType.DMA((4, chips)),
            pltpu.SemaphoreType.DMA((4, chips)),
            pltpu.SemaphoreType.DMA((4, chips)),
            pltpu.SemaphoreType.DMA((4, chips)),
        ],
        compiler_params=pltpu.CompilerParams(
            collective_id=0, has_side_effects=True, vmem_limit_bytes=56 * 2**20
        ),
        name="gather_project",
    )(
        tokens, norm_gain[None, :], query_weight, key_weight, value_weight, cache_keys,
        cache_values, cos_table, sin_table,
    )

    fresh_k = fresh_k.reshape(n * tok_rows, kv_cols)
    fresh_v = fresh_v.reshape(n * tok_rows, kv_cols)
    scalars = jnp.concatenate([cache_lengths, rank.astype(jnp.int32)[None]])
    cache_spec = pl.BlockSpec(
        (1, cache_rows, HEAD_DIM), lambda g, c, s: (jnp.minimum(c, n - 1), 0, g)
    )
    fresh_spec = pl.BlockSpec((n * tok_rows, HEAD_DIM), lambda g, c, s: (0, g))
    rows = group * tok_rows
    return pl.pallas_call(
        functools.partial(attend_kernel, n),
        out_shape=jax.ShapeDtypeStruct((tok_rows, q_cols), bf16),
        grid_spec=pltpu.PrefetchScalarGridSpec(
            num_scalar_prefetch=1,
            grid=(local_kv, n + 1),
            in_specs=[
                pl.BlockSpec((group, tok_rows, HEAD_DIM), lambda g, c, s: (g, 0, 0)),
                cache_spec,
                cache_spec,
                fresh_spec,
                fresh_spec,
            ],
            out_specs=pl.BlockSpec((tok_rows, group * HEAD_DIM), lambda g, c, s: (0, g)),
            scratch_shapes=[
                pltpu.VMEM((HEAD_DIM, rows), jnp.float32),
                pltpu.VMEM((1, rows), jnp.float32),
                pltpu.VMEM((1, rows), jnp.float32),
            ],
        ),
        compiler_params=pltpu.CompilerParams(vmem_limit_bytes=48 * 2**20),
        name="attend",
    )(scalars, q, all_k, all_v, fresh_k, fresh_v)


def solution(mesh):
    in_specs = (
        P("ctx", "head"),
        P(),
        P(None, "head"),
        P(None, "head"),
        P(None, "head"),
        P("ctx", "head"),
        P("ctx", "head"),
        P(),
        P(),
    )
    out_specs = P("ctx", "head")
    return jax.shard_map(body, mesh=mesh, in_specs=in_specs, out_specs=out_specs, check_vma=False)
```
